1024 devices in a mesh: dom: 256 (over z_hi, x, y, core), rep: 4 (over z_lo).
Axes of the slice: x: 8, y: 8, z: 8 (z_hi: 2, z_lo: 4; z = z_hi * 4 + z_lo), core: 2. Of those that a mesh axis runs over, the one named last changes fastest.
Arguments:
- features: bfloat16 [262144, 256], P(('dom', 'rep')), may hold values from -6 to 6
- tile_values: bfloat16 [2048, 20, 128, 128], P(('dom', 'rep')), may hold values from -0.4375 to 0.4375
- tile_cols: int32 [2048, 20], P(('dom', 'rep')), may hold values from 0 to 39
- tile_counts: int32 [2048], P(('dom', 'rep')), may hold values from 1 to 20, as said below
- weight: bfloat16 [256, 256], replicated, may hold values from -0.375 to 0.375
- cotangent: bfloat16 [262144, 256], P(('dom', 'rep')), may hold values from -6 to 6
Outputs:
- layer_out: bfloat16 [262144, 256], P(('dom', 'rep'))
- feat_grad: float32 [262144, 256], P(('dom', 'rep'))
- weight_grad: float32 [256, 256], replicated
The draws below stay inside these ranges and needn't reach their ends.
Inputs may be any that keep to these rules, and one draw needn't show every extreme that they name: `tile_counts`: in every aligned block of 4 rows of tiles at least one row holds 20 live slots; other rows are skewed towards few slots.
All inputs are finite; a program needn't handle non-finite values.
Results may differ from the reference program's by a relative error of at most 0.0065.
Values may be sent and summed in bfloat16 or wider, within the bound.
No kernel may reach another device: no remote copies, remote signals or barrier semaphores. Data moves between devices by JAX's collectives and lax.ppermute only.
A program may use at most 64 MiB of HBM per device.

```python
import math
import jax
import jax.numpy as jnp
from jax import lax

F = 256
ROWS_DEV = 256
TSLOT = 20
REACH = 2
NODES = 262144
BANDT = 40
N_DOM = 256
N_REP = 4


def draw_tile_counts(key, part):
    key = jax.random.fold_in(key, 7)
    first, second, third = jax.random.split(key, 3)
    rows = NODES // 128
    base = jnp.minimum(jax.random.randint(first, (rows,), 1, TSLOT + 1), jax.random.randint(second, (rows,), 1, TSLOT + 1))
    position = jax.random.randint(third, (rows // 4,), 0, 4)
    full = jnp.arange(rows) % 4 == jnp.repeat(position, 4)
    return jnp.where(full, TSLOT, base).astype(jnp.int32)


def set_ends(result, key, least, high):
    longest = result.shape.index(max(result.shape))
    spots = []
    for shift in (0, 1):
        where = [jax.random.randint(jax.random.fold_in(key, axis), (), 0, length) for axis, length in enumerate(result.shape)]
        where[longest] = (where[longest] + shift) % result.shape[longest]
        spots.append(tuple(where))
    return result.at[spots[0]].set(least).at[spots[1]].set(high)


def block_levels(stream_key, dims, pieces, least, top_value):
    gain, own = 1.0, jax.random.fold_in(stream_key, 6)
    for axis_at, parts in pieces:
        steps = jnp.exp(jax.random.uniform(jax.random.fold_in(own, axis_at), (parts,), jnp.float32, least / len(pieces), top_value / len(pieces)))
        gain = gain * jnp.repeat(steps, dims[axis_at] // parts).reshape([-1 if axis == axis_at else 1 for axis in range(len(dims))])
    return gain


def normal_values(own_key, dims, scale, most, shards=(), held_as=jnp.bfloat16):
    drawn = jax.random.normal(own_key, dims, jnp.float32) * scale
    if len(shards) > 0:
        drawn = block_levels(own_key, dims, shards, -0.22, 0.18) * drawn
    return jnp.clip(drawn, min=-most, max=most).astype(held_as)


def setup_inputs(seed: int = 0) -> dict:
    streams_of = jax.random.split(jax.random.key(seed), 7)
    features = normal_values(streams_of[0], (NODES, F), 1.0, 6.0, ((0, 1024),))
    tile_values = normal_values(streams_of[1], (NODES // 128, TSLOT, 128, 128), ((64 * TSLOT) ** -0.5), 0.4375, ((0, 1024),))
    tile_cols = set_ends(jax.random.randint(streams_of[2], (NODES // 128, TSLOT), 0, BANDT), jax.random.fold_in(streams_of[2], 1), 0, BANDT - 1).astype(jnp.int32)
    tile_counts = draw_tile_counts(jax.random.fold_in(streams_of[6], 71), 0)
    weight = normal_values(streams_of[4], (F, F), F ** -0.5, 0.375)
    cotangent = normal_values(streams_of[5], (NODES, F), 1.0, 6.0, ((0, 1024),))
    return dict(features=features, tile_values=tile_values, tile_cols=tile_cols, tile_counts=tile_counts, weight=weight, cotangent=cotangent)


def reference(features, tile_values, tile_cols, tile_counts, weight, cotangent):
    tile_rows = NODES // 128
    per_group = ROWS_DEV * N_REP // 128
    block = 32
    steps_count = tile_rows // block
    tile_index = jnp.arange(tile_rows, dtype=jnp.int32)
    group_of = tile_index // per_group
    band_block = tile_cols // per_group
    within = tile_cols % per_group
    gcol = ((group_of[:, None] + band_block - REACH) % N_DOM * per_group + within).astype(jnp.int32)
    live = jnp.arange(TSLOT, dtype=jnp.int32)[None, :] < tile_counts[:, None]
    x_tiles = features.reshape(tile_rows, 128, F)
    values_blocks = tile_values.reshape(steps_count, block, TSLOT, 128, 128)
    gcol_blocks = gcol.reshape(steps_count, block, TSLOT)
    live_blocks = live.reshape(steps_count, block, TSLOT)

    def masked_of(values, lives):
        return jnp.where(lives[:, :, None, None], values, jnp.zeros_like(values))

    def forward_block(args):
        values, cols, lives = args
        masked = masked_of(values, lives).astype(jnp.float32)
        picked = x_tiles[cols].astype(jnp.float32)
        return jnp.einsum('tsij,tsjf->tif', masked, picked)
    aggregated = lax.map(forward_block, (values_blocks, gcol_blocks, live_blocks))
    aggregated = aggregated.reshape(NODES, F).astype(jnp.bfloat16)
    layer_out = jnp.dot(aggregated, weight, preferred_element_type=jnp.float32).astype(jnp.bfloat16)
    weight_grad = jnp.dot(aggregated.T, cotangent, preferred_element_type=jnp.float32) / math.sqrt(NODES)
    back = jnp.dot(cotangent, weight.T, preferred_element_type=jnp.float32).astype(jnp.bfloat16)
    back_blocks = back.reshape(steps_count, block, 128, F)

    def backward_step(total, args):
        values, cols, lives, rows_back = args
        masked = masked_of(values, lives).astype(jnp.float32)
        spread = jnp.einsum('tsji,tjf->tsif', masked, rows_back.astype(jnp.float32))
        total = total.at[cols.reshape(-1)].add(spread.reshape(-1, 128, F))
        return (total, None)
    start = jnp.zeros((tile_rows, 128, F), jnp.float32)
    total, unused = lax.scan(backward_step, start, (values_blocks, gcol_blocks, live_blocks, back_blocks))
    feat_grad = total.reshape(NODES, F)
    return (layer_out, feat_grad, weight_grad)
```

```python
import functools
import math

import jax
import jax.numpy as jnp
from jax import lax
from jax.experimental import pallas as pl
from jax.experimental.pallas import tpu as pltpu
from jax.sharding import Mesh, PartitionSpec as P

TILE = 128
ALL = ("zh", "x", "y", "c", "zl")
DOM = ("zh", "x", "y", "c")
PLANE = ("x", "y")
COLUMN = ("zh", "zl", "c")
VMEM_LIMIT = 24 * 1024 * 1024


def near_pairs(groups):
    pairs = []
    for d in range(groups):
        k, c = d // 2, d % 2
        pairs.append((d, (2 * (k - 1) + 1 if c == 0 else 2 * (k + 1)) % groups))
    return pairs


def far_pairs(groups, outward):
    pairs = []
    for d in range(groups):
        step = 2 if (d % 2 == 1) == outward else -2
        pairs.append((d, (d + step) % groups))
    return pairs


def tile_of(col, core, per_group):
    band = col // per_group
    band = jnp.where(core == 0, 4 - band, band)
    place = jnp.where(band >= 2, band - 2, 4 - band)
    return place * per_group + col % per_group


def forward_kernel(core_ref, counts, cols, tiles, weight, cotangent, x0, x1, x2, x3, x4, out, local, band, sems):
    sources = (x0, x1, x2, x3, x4)
    rows = x0.shape[0]
    per_group = rows // TILE
    copies = []
    for index, source in enumerate(sources):
        copy = pltpu.make_async_copy(source, band.at[pl.ds(index * rows, rows)], sems.at[index])
        copy.start()
        copies.append(copy)
    for copy in copies:
        copy.wait()
    core = core_ref[0]
    slots = tiles.shape[1]
    sums = []
    for t in range(tiles.shape[0]):
        count = counts[t]
        total = jnp.zeros((TILE, x0.shape[1]), jnp.float32)
        for s in range(0, slots, 2):
            left, right = [], []
            for one in (s, s + 1):
                start = pl.multiple_of(tile_of(cols[t, one], core, per_group) * TILE, TILE)
                value = tiles[t, one]
                left.append(jnp.where(one < count, value, jnp.zeros_like(value)))
                right.append(band[pl.ds(start, TILE), :])
            total = total + jnp.dot(
                jnp.concatenate(left, 1), jnp.concatenate(right, 0), preferred_element_type=jnp.float32
            )
        sums.append(total.astype(jnp.bfloat16))
    aggregated = jnp.concatenate(sums, 0)
    out[...] = jnp.dot(aggregated, weight[...], preferred_element_type=jnp.float32).astype(jnp.bfloat16)
    grad = lax.dot_general(
        aggregated, cotangent[...], (((0,), (0,)), ((), ())), preferred_element_type=jnp.float32
    ).astype(jnp.bfloat16)
    height = grad.shape[0]
    local[0:height, :] = grad[:, 0:TILE]
    local[height : 2 * height, :] = grad[:, TILE : 2 * TILE]


def scatter_tiles(core, counts, cols, tiles, cotangent, total, least, most, per_group):
    for t in range(tiles.shape[0]):
        grads = cotangent[t * TILE : (t + 1) * TILE, :]

        def step(s, carry):
            place = tile_of(cols[t, s], core, per_group)

            @pl.when((place >= least) & (place < most))
            def _():
                start = pl.multiple_of((place - least) * TILE, TILE)
                total[pl.ds(start, TILE), :] += lax.dot_general(
                    tiles[t, s], grads, (((0,), (0,)), ((), ())), preferred_element_type=jnp.float32
                )

            return carry

        lax.fori_loop(0, counts[t], step, 0)


def send_kernel(core_ref, counts, cols, tiles, cotangent, out, total):
    per_group = out.shape[0] // TILE // 2
    total[...] = jnp.zeros_like(total)
    scatter_tiles(core_ref[0], counts, cols, tiles, cotangent, total, 3 * per_group, 5 * per_group, per_group)
    out[...] = total[...].astype(jnp.bfloat16)


def keep_kernel(core_ref, counts, cols, tiles, cotangent, received, own, near, far, total):
    rows = own.shape[0]
    per_group = rows // TILE
    total[0 : 2 * rows, :] = received[...].astype(jnp.float32)
    total[2 * rows : 3 * rows, :] = jnp.zeros_like(total[2 * rows : 3 * rows, :])
    scatter_tiles(core_ref[0], counts, cols, tiles, cotangent, total, 0, 3 * per_group, per_group)
    own[...] = total[0:rows, :]
    near[...] = total[rows : 2 * rows, :].astype(jnp.bfloat16)
    far[...] = total[2 * rows : 3 * rows, :].astype(jnp.bfloat16)


def params():
    return pltpu.CompilerParams(vmem_limit_bytes=VMEM_LIMIT)


def per_device(features, tile_values, tile_cols, tile_counts, weight, cotangent):
    rows, width = features.shape
    slots = tile_cols.shape[1]
    groups = math.prod(lax.axis_size(axis) for axis in DOM)
    members = lax.axis_size("zl")
    group_rows = rows * members
    core = lax.axis_index("c").astype(jnp.int32).reshape(1)
    near = near_pairs(groups)
    swap = [(0, 1), (1, 0)]
    smem = pl.BlockSpec(memory_space=pltpu.SMEM)
    vmem = pl.BlockSpec(memory_space=pltpu.VMEM)
    anywhere = pl.BlockSpec(memory_space=pl.ANY)
    flops = 2 * 2 * slots * TILE * TILE * width

    x0 = lax.all_gather(features, "zl", axis=0, tiled=True)
    x1 = lax.ppermute(x0, DOM, near)
    x2 = lax.ppermute(x0, DOM, far_pairs(groups, False))
    x3 = lax.ppermute(x0, "c", swap)
    x4 = lax.ppermute(x1, "c", swap)

    sent = pl.pallas_call(
        send_kernel,
        out_shape=jax.ShapeDtypeStruct((2 * group_rows, width), jnp.bfloat16),
        in_specs=[smem, smem, smem, vmem, vmem],
        out_specs=vmem,
        scratch_shapes=[pltpu.VMEM((2 * group_rows, width), jnp.float32)],
        compiler_params=params(),
        cost_estimate=pl.CostEstimate(flops=flops, bytes_accessed=4 << 20, transcendentals=0),
        name="send",
    )(core, tile_counts, tile_cols, tile_values, cotangent)
    received = lax.ppermute(sent, "c", swap)
    own, near_sum, far_sum = pl.pallas_call(
        keep_kernel,
        out_shape=(
            jax.ShapeDtypeStruct((group_rows, width), jnp.float32),
            jax.ShapeDtypeStruct((group_rows, width), jnp.bfloat16),
            jax.ShapeDtypeStruct((group_rows, width), jnp.bfloat16),
        ),
        in_specs=[smem, smem, smem, vmem, vmem, vmem],
        out_specs=(vmem, vmem, vmem),
        scratch_shapes=[pltpu.VMEM((3 * group_rows, width), jnp.float32)],
        compiler_params=params(),
        cost_estimate=pl.CostEstimate(flops=flops, bytes_accessed=8 << 20, transcendentals=0),
        name="keep",
    )(core, tile_counts, tile_cols, tile_values, cotangent, received)
    near_in = lax.ppermute(near_sum, DOM, near)
    far_in = lax.ppermute(far_sum, DOM, far_pairs(groups, True))

    layer_out, local = pl.pallas_call(
        forward_kernel,
        out_shape=(
            jax.ShapeDtypeStruct((rows, width), jnp.bfloat16),
            jax.ShapeDtypeStruct((2 * width, TILE), jnp.bfloat16),
        ),
        in_specs=[smem, smem, smem, vmem, vmem, vmem] + [anywhere] * 5,
        out_specs=(vmem, vmem),
        scratch_shapes=[
            pltpu.VMEM((5 * group_rows, width), jnp.bfloat16),
            pltpu.SemaphoreType.DMA((5,)),
        ],
        compiler_params=params(),
        cost_estimate=pl.CostEstimate(flops=flops, bytes_accessed=6 << 20, transcendentals=0),
        name="forward",
    )(core, tile_counts, tile_cols, tile_values, weight, cotangent, x0, x1, x2, x3, x4)

    plane = math.prod(lax.axis_size(axis) for axis in PLANE)
    column = math.prod(lax.axis_size(axis) for axis in COLUMN)
    parts = lax.all_to_all(local.reshape(plane, -1, TILE), PLANE, 0, 0)
    part = jnp.sum(parts.astype(jnp.float32), 0)
    parts = lax.all_to_all(jnp.broadcast_to(part[None], (column,) + part.shape), COLUMN, 0, 0)
    part = jnp.sum(parts, 0) / math.sqrt(rows * groups * members)
    part = part.astype(jnp.bfloat16)
    parts = lax.all_to_all(jnp.broadcast_to(part[None], (plane,) + part.shape), PLANE, 0, 0)
    parts = parts.reshape(2, width, TILE).astype(jnp.float32)
    weight_grad = jnp.concatenate([parts[0], parts[1]], 1)

    total = (own + near_in.astype(jnp.float32) + far_in.astype(jnp.float32)).astype(jnp.bfloat16)
    mine = lax.psum_scatter(total, "zl", scatter_dimension=0, tiled=True)
    feat_grad = lax.dot_general(mine, weight, (((1,), (1,)), ((), ())), preferred_element_type=jnp.float32)
    return (layer_out, feat_grad, weight_grad)


def solution(mesh):
    split = Mesh(mesh.devices.reshape(2, 8, 8, 2, 4), ALL)
    rows = P(ALL)
    return jax.shard_map(
        per_device,
        mesh=split,
        in_specs=(rows, rows, rows, rows, P(), rows),
        out_specs=(rows, rows, P()),
        check_vma=False,
    )
```

```python
import functools
import math

import jax
import jax.numpy as jnp
from jax import lax
from jax.experimental import pallas as pl
from jax.experimental.pallas import tpu as pltpu
from jax.sharding import Mesh, PartitionSpec as P

TILE = 128
ALL = ("zh", "x", "y", "c", "zl")
DOM = ("zh", "x", "y", "c")
PLANE = ("x", "y")
COLUMN = ("zh", "zl", "c")
SEND_BYTES = 64 << 20
FORWARD_BYTES = 64 << 20
VMEM_LIMIT = 24 * 1024 * 1024


def near_pairs(groups):
    pairs = []
    for d in range(groups):
        k, c = d // 2, d % 2
        pairs.append((d, (2 * (k - 1) + 1 if c == 0 else 2 * (k + 1)) % groups))
    return pairs


def far_pairs(groups, outward):
    pairs = []
    for d in range(groups):
        step = 2 if (d % 2 == 1) == outward else -2
        pairs.append((d, (d + step) % groups))
    return pairs


def tile_of(col, core, per_group):
    band = col // per_group
    band = jnp.where(core == 0, 4 - band, band)
    place = jnp.where(band >= 2, band - 2, 4 - band)
    return place * per_group + col % per_group


def turned_tile_of(col, core, member, members, per_group):
    tile = tile_of(col, core, per_group)
    share = per_group // members
    within = tile % per_group
    turn = (member - within // share + members) % members
    return tile - within + turn * share + within % share


def forward_kernel(place_ref, counts, cols, tiles, weight, mine, turn1, turn2, turn3, other, out, band, sems):
    turns = (mine, turn1, turn2, turn3)
    members = len(turns)
    rows = mine.shape[0] // 3
    group_rows = rows * members
    per_group = group_rows // TILE
    sources = []
    for index, turn in enumerate(turns):
        for place in range(3):
            sources.append((turn.at[pl.ds(place * rows, rows)], place * group_rows + index * rows, rows))
    sources.append((other, 3 * group_rows, 2 * group_rows))
    copies = []
    for index, (source, start, size) in enumerate(sources):
        copy = pltpu.make_async_copy(source, band.at[pl.ds(start, size)], sems.at[index])
        copy.start()
        copies.append(copy)
    for copy in copies:
        copy.wait()
    member = place_ref[1]
    width = mine.shape[1]
    core = place_ref[0]
    slots = tiles.shape[1]
    sums = []
    for t in range(tiles.shape[0]):
        count = counts[t]
        total = jnp.zeros((TILE, width), jnp.float32)
        for s in range(0, slots, 2):
            left, right = [], []
            for one in (s, s + 1):
                start = pl.multiple_of(turned_tile_of(cols[t, one], core, member, members, per_group) * TILE, TILE)
                value = tiles[t, one]
                left.append(jnp.where(one < count, value, jnp.zeros_like(value)))
                right.append(band[pl.ds(start, TILE), :])
            total = total + jnp.dot(
                jnp.concatenate(left, 1), jnp.concatenate(right, 0), preferred_element_type=jnp.float32
            )
        sums.append(total.astype(jnp.bfloat16))
    aggregated = jnp.concatenate(sums, 0)
    out[...] = jnp.dot(aggregated, weight[...], preferred_element_type=jnp.float32).astype(jnp.bfloat16)


def scatter_tiles(core, counts, cols, tiles, cotangent, total, least, most, per_group):
    for t in range(tiles.shape[0]):
        grads = cotangent[t * TILE : (t + 1) * TILE, :]

        def step(s, carry):
            place = tile_of(cols[t, s], core, per_group)

            @pl.when((place >= least) & (place < most))
            def _():
                start = pl.multiple_of((place - least) * TILE, TILE)
                total[pl.ds(start, TILE), :] += lax.dot_general(
                    tiles[t, s], grads, (((0,), (0,)), ((), ())), preferred_element_type=jnp.float32
                )

            return carry

        lax.fori_loop(0, counts[t], step, 0)


def send_kernel(place_ref, counts, cols, tiles, cotangent, out, total):
    per_group = out.shape[0] // TILE // 2
    total[...] = jnp.zeros_like(total)
    scatter_tiles(place_ref[0], counts, cols, tiles, cotangent, total, 3 * per_group, 5 * per_group, per_group)
    out[...] = total[...].astype(jnp.bfloat16)


def keep_kernel(place_ref, counts, cols, tiles, cotangent, received, features, out, passed, total):
    passed[...] = features[...]
    members, blocks, rows, _ = out.shape
    group_rows = members * rows
    per_group = group_rows // TILE
    total[0 : 2 * group_rows, :] = received[...].astype(jnp.float32)
    total[2 * group_rows : 3 * group_rows, :] = jnp.zeros_like(total[2 * group_rows : 3 * group_rows, :])
    scatter_tiles(place_ref[0], counts, cols, tiles, cotangent, total, 0, 3 * per_group, per_group)
    for m in range(members):
        for b in range(blocks):
            start = b * group_rows + m * rows
            out[m, b] = total[start : start + rows, :].astype(jnp.bfloat16)


def fold_kernel(parts, out):
    part = jnp.sum(parts[...].astype(jnp.float32), 0)
    for i in range(out.shape[0]):
        out[i] = part


def products_kernel(parts, features, near_x, far_x, own, near, far, local, mine):
    total = parts[0].astype(jnp.float32)
    for m in range(1, parts.shape[0]):
        total = total + parts[m].astype(jnp.float32)
    own[...] = total[0]
    rounded = total.astype(jnp.bfloat16)
    near[...] = rounded[1]
    far[...] = rounded[2]
    grad = jnp.zeros((features.shape[1], rounded.shape[2]), jnp.float32)
    for block, rows in enumerate((features, near_x, far_x)):
        grad = grad + lax.dot_general(
            rows[...], rounded[block], (((0,), (0,)), ((), ())), preferred_element_type=jnp.float32
        )
    grad = grad.astype(jnp.bfloat16)
    height = grad.shape[0]
    local[0:height, :] = grad[:, 0:TILE]
    local[height : 2 * height, :] = grad[:, TILE : 2 * TILE]
    size = features.shape[0]
    for index, rows in enumerate((features, near_x, far_x)):
        mine[index * size : (index + 1) * size, :] = rows[...]


def spread_kernel(scale, folded, own, near, far, weight, spread, feat):
    part = (jnp.sum(folded[...], 0) * scale).astype(jnp.bfloat16)
    for i in range(spread.shape[0]):
        spread[i] = part
    total = own[...] + near[...].astype(jnp.float32) + far[...].astype(jnp.float32)
    feat[...] = lax.dot_general(
        total.astype(jnp.bfloat16), weight[...], (((1,), (1,)), ((), ())), preferred_element_type=jnp.float32
    )


def pack_kernel(mine, turn1, turn2, turn3, after, out, sems):
    rows = mine.shape[0] // 3
    turns = (mine, turn1, turn2, turn3)
    copies = []
    for place in range(2):
        for index, turn in enumerate(turns):
            number = place * len(turns) + index
            copy = pltpu.make_async_copy(
                turn.at[pl.ds(place * rows, rows)], out.at[pl.ds(number * rows, rows)], sems.at[number]
            )
            copy.start()
            copies.append(copy)
    for copy in copies:
        copy.wait()


def last_kernel(parts, after, grad):
    count, depth, _ = parts.shape
    height = grad.shape[0]
    half = height // depth
    for side in range(count // half):
        grad[:, side * TILE : (side + 1) * TILE] = (
            parts[side * half : (side + 1) * half].astype(jnp.float32).reshape(height, TILE)
        )


def params():
    return pltpu.CompilerParams(vmem_limit_bytes=VMEM_LIMIT)


def per_device(features, tile_values, tile_cols, tile_counts, weight, cotangent):
    rows, width = features.shape
    slots = tile_cols.shape[1]
    groups = math.prod(lax.axis_size(axis) for axis in DOM)
    members = lax.axis_size("zl")
    group_rows = rows * members
    near = near_pairs(groups)
    swap = [(0, 1), (1, 0)]
    smem = pl.BlockSpec(memory_space=pltpu.SMEM)
    vmem = pl.BlockSpec(memory_space=pltpu.VMEM)
    anywhere = pl.BlockSpec(memory_space=pl.ANY)
    flops = 2 * 2 * slots * TILE * TILE * width

    place = jnp.stack([lax.axis_index("c"), lax.axis_index("zl")]).astype(jnp.int32)

    def turned(value):
        return [
            lax.ppermute(value, "zl", [(m, (m + turn) % members) for m in range(members)]) for turn in range(1, members)
        ]


    sent = pl.pallas_call(
        send_kernel,
        out_shape=jax.ShapeDtypeStruct((2 * group_rows, width), jnp.bfloat16),
        in_specs=[smem, smem, smem, vmem, vmem],
        out_specs=vmem,
        scratch_shapes=[pltpu.VMEM((2 * group_rows, width), jnp.float32)],
        compiler_params=params(),
        cost_estimate=pl.CostEstimate(flops=flops, bytes_accessed=SEND_BYTES, transcendentals=0),
        name="send",
    )(place, tile_counts, tile_cols, tile_values, cotangent)
    received = lax.ppermute(sent, "c", swap)
    kept, passed = pl.pallas_call(
        keep_kernel,
        out_shape=(
            jax.ShapeDtypeStruct((members, 3, rows, width), jnp.bfloat16),
            jax.ShapeDtypeStruct(features.shape, jnp.bfloat16),
        ),
        in_specs=[smem, smem, smem, vmem, vmem, vmem, vmem],
        out_specs=(vmem, vmem),
        scratch_shapes=[pltpu.VMEM((3 * group_rows, width), jnp.float32)],
        compiler_params=params(),
        cost_estimate=pl.CostEstimate(flops=flops, bytes_accessed=8 << 20, transcendentals=0),
        name="keep",
    )(place, tile_counts, tile_cols, tile_values, cotangent, received, features)
    kept = lax.all_to_all(kept, "zl", 0, 0)
    near_x = lax.ppermute(passed, DOM, near)
    far_x = lax.ppermute(passed, DOM, far_pairs(groups, False))

    own, near_sum, far_sum, local, mine = pl.pallas_call(
        products_kernel,
        out_shape=(
            jax.ShapeDtypeStruct((rows, width), jnp.float32),
            jax.ShapeDtypeStruct((rows, width), jnp.bfloat16),
            jax.ShapeDtypeStruct((rows, width), jnp.bfloat16),
            jax.ShapeDtypeStruct((2 * width, TILE), jnp.bfloat16),
            jax.ShapeDtypeStruct((3 * rows, width), jnp.bfloat16),
        ),
        in_specs=[vmem] * 4,
        out_specs=(vmem,) * 5,
        compiler_params=params(),
        cost_estimate=pl.CostEstimate(flops=flops, bytes_accessed=3 << 20, transcendentals=0),
        name="products",
    )(kept, features, near_x, far_x)

    plane = math.prod(lax.axis_size(axis) for axis in PLANE)
    column = math.prod(lax.axis_size(axis) for axis in COLUMN)
    parts = lax.all_to_all(local.reshape(plane, -1, TILE), PLANE, 0, 0)
    near_in = lax.ppermute(near_sum, DOM, near)
    far_in = lax.ppermute(far_sum, DOM, far_pairs(groups, True))
    turns = turned(mine)
    part = pl.pallas_call(
        fold_kernel,
        out_shape=jax.ShapeDtypeStruct((column,) + parts.shape[1:], jnp.float32),
        in_specs=[vmem],
        out_specs=vmem,
        compiler_params=params(),
        name="fold",
    )(parts)
    folded = lax.all_to_all(part, COLUMN, 0, 0)
    spread, feat_grad = pl.pallas_call(
        functools.partial(spread_kernel, 1 / math.sqrt(rows * groups * members)),
        out_shape=(
            jax.ShapeDtypeStruct(parts.shape, jnp.bfloat16),
            jax.ShapeDtypeStruct((rows, width), jnp.float32),
        ),
        in_specs=[vmem] * 5,
        out_specs=(vmem, vmem),
        compiler_params=params(),
        name="spread",
    )(folded, own, near_in, far_in, weight)
    parts = lax.all_to_all(spread, PLANE, 0, 0)
    packed = pl.pallas_call(
        pack_kernel,
        out_shape=jax.ShapeDtypeStruct((2 * group_rows, width), jnp.bfloat16),
        in_specs=[anywhere] * 5,
        out_specs=anywhere,
        scratch_shapes=[pltpu.SemaphoreType.DMA((8,))],
        compiler_params=params(),
        cost_estimate=pl.CostEstimate(flops=0, bytes_accessed=2 << 20, transcendentals=0),
        name="pack",
    )(mine, *turns, parts)
    other = lax.ppermute(packed, "c", swap)
    layer_out = pl.pallas_call(
        forward_kernel,
        out_shape=jax.ShapeDtypeStruct((rows, width), jnp.bfloat16),
        in_specs=[smem, smem, smem, vmem, vmem] + [anywhere] * 5,
        out_specs=vmem,
        scratch_shapes=[
            pltpu.VMEM((5 * group_rows, width), jnp.bfloat16),
            pltpu.SemaphoreType.DMA((13,)),
        ],
        compiler_params=params(),
        cost_estimate=pl.CostEstimate(flops=flops, bytes_accessed=FORWARD_BYTES, transcendentals=0),
        name="forward",
    )(place, tile_counts, tile_cols, tile_values, weight, mine, *turns, other)
    weight_grad = pl.pallas_call(
        last_kernel,
        out_shape=jax.ShapeDtypeStruct(weight.shape, jnp.float32),
        in_specs=[vmem, anywhere],
        out_specs=vmem,
        compiler_params=params(),
        name="last",
    )(parts, layer_out)
    return (layer_out, feat_grad, weight_grad)


def solution(mesh):
    split = Mesh(mesh.devices.reshape(2, 8, 8, 2, 4), ALL)
    rows = P(ALL)
    return jax.shard_map(
        per_device,
        mesh=split,
        in_specs=(rows, rows, rows, rows, P(), rows),
        out_specs=(rows, rows, P()),
        check_vma=False,
    )
```

```python
import functools
import math

import jax
import jax.numpy as jnp
from jax import lax
from jax.experimental import pallas as pl
from jax.experimental.pallas import tpu as pltpu
from jax.sharding import Mesh, PartitionSpec as P

TILE = 128
ALL = ("zh", "x", "y", "c", "zl")
DOM = ("zh", "x", "y", "c")
PLANE = ("x", "y")
COLUMN = ("zh", "zl", "c")
VMEM_LIMIT = 24 * 1024 * 1024


def near_pairs(groups):
    pairs = []
    for d in range(groups):
        k, c = d // 2, d % 2
        pairs.append((d, (2 * (k - 1) + 1 if c == 0 else 2 * (k + 1)) % groups))
    return pairs


def far_pairs(groups, outward):
    pairs = []
    for d in range(groups):
        step = 2 if (d % 2 == 1) == outward else -2
        pairs.append((d, (d + step) % groups))
    return pairs


def tile_of(col, core, per_group):
    band = col // per_group
    band = jnp.where(core == 0, 4 - band, band)
    place = jnp.where(band >= 2, band - 2, 4 - band)
    return place * per_group + col % per_group


def forward_kernel(place_ref, counts, cols, tiles, weight, cotangent, x0, x1, x2, x3, x4, out, local, band, sems):
    sources = (x0, x1, x2, x3, x4)
    rows = x0.shape[0]
    per_group = rows // TILE
    copies = []
    for index, source in enumerate(sources):
        copy = pltpu.make_async_copy(source, band.at[pl.ds(index * rows, rows)], sems.at[index])
        copy.start()
        copies.append(copy)
    for copy in copies:
        copy.wait()
    core = place_ref[0]
    slots = tiles.shape[1]
    sums = []
    for t in range(tiles.shape[0]):
        count = counts[t]
        total = jnp.zeros((TILE, x0.shape[1]), jnp.float32)
        for s in range(0, slots, 2):
            left, right = [], []
            for one in (s, s + 1):
                start = pl.multiple_of(tile_of(cols[t, one], core, per_group) * TILE, TILE)
                value = tiles[t, one]
                left.append(jnp.where(one < count, value, jnp.zeros_like(value)))
                right.append(band[pl.ds(start, TILE), :])
            total = total + jnp.dot(
                jnp.concatenate(left, 1), jnp.concatenate(right, 0), preferred_element_type=jnp.float32
            )
        sums.append(total.astype(jnp.bfloat16))
    aggregated = jnp.concatenate(sums, 0)
    out[...] = jnp.dot(aggregated, weight[...], preferred_element_type=jnp.float32).astype(jnp.bfloat16)
    grad = lax.dot_general(
        aggregated, cotangent[...], (((0,), (0,)), ((), ())), preferred_element_type=jnp.float32
    )
    height = grad.shape[0]
    local[0:height, :] = grad[:, 0:TILE]
    local[height : 2 * height, :] = grad[:, TILE : 2 * TILE]


def scatter_tiles(core, counts, cols, tiles, cotangent, total, least, most, per_group):
    for t in range(tiles.shape[0]):
        grads = cotangent[t * TILE : (t + 1) * TILE, :]

        def step(s, carry):
            place = tile_of(cols[t, s], core, per_group)

            @pl.when((place >= least) & (place < most))
            def _():
                start = pl.multiple_of((place - least) * TILE, TILE)
                total[pl.ds(start, TILE), :] += lax.dot_general(
                    tiles[t, s], grads, (((0,), (0,)), ((), ())), preferred_element_type=jnp.float32
                )

            return carry

        lax.fori_loop(0, counts[t], step, 0)


def send_kernel(place_ref, counts, cols, tiles, cotangent, after, out, total):
    per_group = out.shape[0] // TILE // 2
    total[...] = jnp.zeros_like(total)
    scatter_tiles(place_ref[0], counts, cols, tiles, cotangent, total, 3 * per_group, 5 * per_group, per_group)
    out[...] = total[...].astype(jnp.bfloat16)


def keep_kernel(place_ref, counts, cols, tiles, cotangent, received, after, own, near, far, total):
    rows = own.shape[0]
    per_group = rows // TILE
    total[0 : 2 * rows, :] = received[...].astype(jnp.float32)
    total[2 * rows : 3 * rows, :] = jnp.zeros_like(total[2 * rows : 3 * rows, :])
    scatter_tiles(place_ref[0], counts, cols, tiles, cotangent, total, 0, 3 * per_group, per_group)
    own[...] = total[0:rows, :]
    near[...] = total[rows : 2 * rows, :].astype(jnp.bfloat16)
    far[...] = total[2 * rows : 3 * rows, :].astype(jnp.bfloat16)


def fold_kernel(parts, out):
    part = jnp.sum(parts[...].astype(jnp.float32), 0)
    for i in range(out.shape[0]):
        out[i] = part


def spread_kernel(scale, folded, spread):
    part = (jnp.sum(folded[...], 0) * scale).astype(jnp.bfloat16)
    for i in range(spread.shape[0]):
        spread[i] = part


def meet_kernel(place_ref, own, near, far, mine, turn1, turn2, turn3):
    rows = mine.shape[0]
    turns = (turn1, turn2, turn3)
    members = len(turns) + 1
    for turn in range(members):
        member = place_ref[1] + turn
        member = jnp.where(member >= members, member - members, member)
        part = pl.ds(pl.multiple_of(member * rows, rows), rows)
        total = own[part, :] + near[part, :].astype(jnp.float32) + far[part, :].astype(jnp.float32)
        if turn == 0:
            mine[...] = total
        else:
            turns[turn - 1][...] = total.astype(jnp.bfloat16)


def last_kernel(mine, turn1, turn2, turn3, weight, parts, feat, grad):
    total = mine[...]
    for turn in (turn1, turn2, turn3):
        total = total + turn[...].astype(jnp.float32)
    feat[...] = lax.dot_general(
        total.astype(jnp.bfloat16), weight[...], (((1,), (1,)), ((), ())), preferred_element_type=jnp.float32
    )
    count, depth, _ = parts.shape
    height = grad.shape[0]
    half = height // depth
    for side in range(count // half):
        grad[:, side * TILE : (side + 1) * TILE] = (
            parts[side * half : (side + 1) * half].astype(jnp.float32).reshape(height, TILE)
        )


def params():
    return pltpu.CompilerParams(vmem_limit_bytes=VMEM_LIMIT)


def per_device(features, tile_values, tile_cols, tile_counts, weight, cotangent):
    rows, width = features.shape
    slots = tile_cols.shape[1]
    groups = math.prod(lax.axis_size(axis) for axis in DOM)
    members = lax.axis_size("zl")
    group_rows = rows * members
    core = jnp.stack([lax.axis_index("c"), lax.axis_index("zl")]).astype(jnp.int32)
    near = near_pairs(groups)
    swap = [(0, 1), (1, 0)]
    smem = pl.BlockSpec(memory_space=pltpu.SMEM)
    vmem = pl.BlockSpec(memory_space=pltpu.VMEM)
    anywhere = pl.BlockSpec(memory_space=pl.ANY)
    flops = 2 * 2 * slots * TILE * TILE * width

    x0 = lax.all_gather(features, "zl", axis=0, tiled=True)
    x1 = lax.ppermute(x0, DOM, near)
    x2 = lax.ppermute(x0, DOM, far_pairs(groups, False))
    x3 = lax.ppermute(x0, "c", swap)
    x4 = lax.ppermute(x1, "c", swap)

    sent = pl.pallas_call(
        send_kernel,
        out_shape=jax.ShapeDtypeStruct((2 * group_rows, width), jnp.bfloat16),
        in_specs=[smem, smem, smem, vmem, vmem, anywhere],
        out_specs=vmem,
        scratch_shapes=[pltpu.VMEM((2 * group_rows, width), jnp.float32)],
        compiler_params=params(),
        cost_estimate=pl.CostEstimate(flops=flops, bytes_accessed=4 << 20, transcendentals=0),
        name="send",
    )(core, tile_counts, tile_cols, tile_values, cotangent, x0)
    received = lax.ppermute(sent, "c", swap)

    layer_out, local = pl.pallas_call(
        forward_kernel,
        out_shape=(
            jax.ShapeDtypeStruct((rows, width), jnp.bfloat16),
            jax.ShapeDtypeStruct((2 * width, TILE), jnp.float32),
        ),
        in_specs=[smem, smem, smem, vmem, vmem, vmem] + [anywhere] * 5,
        out_specs=(vmem, vmem),
        scratch_shapes=[
            pltpu.VMEM((5 * group_rows, width), jnp.bfloat16),
            pltpu.SemaphoreType.DMA((5,)),
        ],
        compiler_params=params(),
        cost_estimate=pl.CostEstimate(flops=flops, bytes_accessed=6 << 20, transcendentals=0),
        name="forward",
    )(core, tile_counts, tile_cols, tile_values, weight, cotangent, x0, x1, x2, x3, x4)

    own, near_sum, far_sum = pl.pallas_call(
        keep_kernel,
        out_shape=(
            jax.ShapeDtypeStruct((group_rows, width), jnp.float32),
            jax.ShapeDtypeStruct((group_rows, width), jnp.bfloat16),
            jax.ShapeDtypeStruct((group_rows, width), jnp.bfloat16),
        ),
        in_specs=[smem, smem, smem, vmem, vmem, vmem, anywhere],
        out_specs=(vmem, vmem, vmem),
        scratch_shapes=[pltpu.VMEM((3 * group_rows, width), jnp.float32)],
        compiler_params=params(),
        cost_estimate=pl.CostEstimate(flops=flops, bytes_accessed=8 << 20, transcendentals=0),
        name="keep",
    )(core, tile_counts, tile_cols, tile_values, cotangent, received, local)
    near_in = lax.ppermute(near_sum, DOM, near)
    far_in = lax.ppermute(far_sum, DOM, far_pairs(groups, True))

    plane = math.prod(lax.axis_size(axis) for axis in PLANE)
    column = math.prod(lax.axis_size(axis) for axis in COLUMN)
    parts = lax.all_to_all(local.reshape(plane, -1, TILE), PLANE, 0, 0)
    part = pl.pallas_call(
        fold_kernel,
        out_shape=jax.ShapeDtypeStruct((column,) + parts.shape[1:], jnp.float32),
        in_specs=[vmem],
        out_specs=vmem,
        compiler_params=params(),
        cost_estimate=pl.CostEstimate(flops=0, bytes_accessed=1 << 20, transcendentals=0),
        name="fold",
    )(parts)
    folded = lax.all_to_all(part, COLUMN, 0, 0)
    mine, *turns = pl.pallas_call(
        meet_kernel,
        out_shape=(jax.ShapeDtypeStruct((rows, width), jnp.float32),)
        + (jax.ShapeDtypeStruct((rows, width), jnp.bfloat16),) * (members - 1),
        in_specs=[smem] + [vmem] * 3,
        out_specs=(vmem,) * members,
        compiler_params=params(),
        name="meet",
    )(core, own, near_in, far_in)
    turns = [
        lax.ppermute(value, "zl", [(m, (m + turn + 1) % members) for m in range(members)])
        for turn, value in enumerate(turns)
    ]
    spread = pl.pallas_call(
        functools.partial(spread_kernel, 1 / math.sqrt(rows * groups * members)),
        out_shape=jax.ShapeDtypeStruct(parts.shape, jnp.bfloat16),
        in_specs=[vmem],
        out_specs=vmem,
        compiler_params=params(),
        name="spread",
    )(folded)
    parts = lax.all_to_all(spread, PLANE, 0, 0)
    feat_grad, weight_grad = pl.pallas_call(
        last_kernel,
        out_shape=(
            jax.ShapeDtypeStruct((rows, width), jnp.float32),
            jax.ShapeDtypeStruct(weight.shape, jnp.float32),
        ),
        in_specs=[vmem] * (members + 2),
        out_specs=(vmem, vmem),
        compiler_params=params(),
        name="last",
    )(mine, *turns, weight, parts)
    return (layer_out, feat_grad, weight_grad)


def solution(mesh):
    split = Mesh(mesh.devices.reshape(2, 8, 8, 2, 4), ALL)
    rows = P(ALL)
    return jax.shard_map(
        per_device,
        mesh=split,
        in_specs=(rows, rows, rows, rows, P(), rows),
        out_specs=(rows, rows, P()),
        check_vma=False,
    )
```

```python
import functools
import math

import jax
import jax.numpy as jnp
from jax import lax
from jax.experimental import pallas as pl
from jax.experimental.pallas import tpu as pltpu
from jax.sharding import Mesh, PartitionSpec as P

TILE = 128
ALL = ("zh", "x", "y", "c", "zl")
DOM = ("zh", "x", "y", "c")
PLANE = ("x", "y")
COLUMN = ("zh", "zl", "c")
VMEM_LIMIT = 24 * 1024 * 1024


def near_pairs(groups):
    pairs = []
    for d in range(groups):
        k, c = d // 2, d % 2
        pairs.append((d, (2 * (k - 1) + 1 if c == 0 else 2 * (k + 1)) % groups))
    return pairs


def far_pairs(groups, outward):
    pairs = []
    for d in range(groups):
        step = 2 if (d % 2 == 1) == outward else -2
        pairs.append((d, (d + step) % groups))
    return pairs


def split_pairs(pairs):
    part = len(pairs) // 2
    inside = [(a, b) for a, b in pairs if a // part == b // part]
    across = [(a, b) for a, b in pairs if a // part != b // part]
    return inside, across


def edge_devices(groups):
    part = groups // 2
    return [d for d in range(groups) if d % part in (0, part - 1)]


def tile_of(col, core, per_group):
    band = col // per_group
    band = jnp.where(core == 0, 4 - band, band)
    place = jnp.where(band >= 2, band - 2, 4 - band)
    return place * per_group + col % per_group


def turned_tile_of(col, core, member, members, per_group):
    tile = tile_of(col, core, per_group)
    share = per_group // members
    within = tile % per_group
    turn = (member - within // share + members) % members
    return tile - within + turn * share + within % share


def forward_kernel(
    members, place_ref, counts, cols, tiles, weight, cotangent, x0, x1, x2, x3, x4, out, local, band, sems
):
    rows = x0.shape[0]
    per_group = rows // TILE
    copies = []
    for index, source in enumerate((x0, x1, x2, x3, x4)):
        copy = pltpu.make_async_copy(source, band.at[pl.ds(index * rows, rows)], sems.at[index])
        copy.start()
        copies.append(copy)
    for copy in copies:
        copy.wait()
    core, member = place_ref[0], place_ref[1]
    slots = tiles.shape[1]
    sums = []
    for t in range(tiles.shape[0]):
        count = counts[t]
        total = jnp.zeros((TILE, x0.shape[1]), jnp.float32)
        for s in range(0, slots, 2):
            left, right = [], []
            for one in (s, s + 1):
                tile = turned_tile_of(cols[t, one], core, member, members, per_group)
                start = pl.multiple_of(tile * TILE, TILE)
                value = tiles[t, one]
                left.append(jnp.where(one < count, value, jnp.zeros_like(value)))
                right.append(band[pl.ds(start, TILE), :])
            total = total + jnp.dot(
                jnp.concatenate(left, 1), jnp.concatenate(right, 0), preferred_element_type=jnp.float32
            )
        sums.append(total.astype(jnp.bfloat16))
    aggregated = jnp.concatenate(sums, 0)
    out[...] = jnp.dot(aggregated, weight[...], preferred_element_type=jnp.float32).astype(jnp.bfloat16)
    grad = lax.dot_general(
        aggregated, cotangent[...], (((0,), (0,)), ((), ())), preferred_element_type=jnp.float32
    )
    height = grad.shape[0]
    local[0:height, :] = grad[:, 0:TILE]
    local[height : 2 * height, :] = grad[:, TILE : 2 * TILE]


def scatter_tiles(core, counts, cols, tiles, cotangent, total, least, most, per_group):
    for t in range(tiles.shape[0]):
        grads = cotangent[t * TILE : (t + 1) * TILE, :]

        def step(s, carry):
            place = tile_of(cols[t, s], core, per_group)

            @pl.when((place >= least) & (place < most))
            def _():
                start = pl.multiple_of((place - least) * TILE, TILE)
                total[pl.ds(start, TILE), :] += lax.dot_general(
                    tiles[t, s], grads, (((0,), (0,)), ((), ())), preferred_element_type=jnp.float32
                )

            return carry

        lax.fori_loop(0, counts[t], step, 0)


def send_kernel(place_ref, counts, cols, tiles, cotangent, after, out, total):
    per_group = out.shape[0] // TILE // 2
    total[...] = jnp.zeros_like(total)
    scatter_tiles(place_ref[0], counts, cols, tiles, cotangent, total, 3 * per_group, 5 * per_group, per_group)
    out[...] = total[...].astype(jnp.bfloat16)


def keep_kernel(
    place_ref, counts, cols, tiles, cotangent, received, after, own, near, far, chunk0, chunk1, chunk2, chunk3, total
):
    rows = own.shape[0]
    per_group = rows // TILE
    total[0 : 2 * rows, :] = received[...].astype(jnp.float32)
    total[2 * rows : 3 * rows, :] = jnp.zeros_like(total[2 * rows : 3 * rows, :])
    scatter_tiles(place_ref[0], counts, cols, tiles, cotangent, total, 0, 3 * per_group, per_group)
    own[...] = total[0:rows, :]
    near[...] = total[rows : 2 * rows, :].astype(jnp.bfloat16)
    far[...] = total[2 * rows : 3 * rows, :].astype(jnp.bfloat16)
    chunks = (chunk0, chunk1, chunk2, chunk3)
    size = chunk0.shape[0] // 2

    @pl.when(place_ref[2] == 1)
    def _():
        for turn, chunk in enumerate(chunks):
            member = place_ref[1] + turn
            member = jnp.where(member >= len(chunks), member - len(chunks), member)
            for index in (1, 2):
                start = pl.multiple_of(index * rows + member * size, size)
                chunk[(index - 1) * size : index * size, :] = total[pl.ds(start, size), :].astype(jnp.bfloat16)

    @pl.when(place_ref[2] == 0)
    def _():
        for chunk in chunks:
            chunk[...] = jnp.zeros_like(chunk)


def cross_kernel(chunk, turn1, turn2, turn3, near, far):
    total = chunk[...].astype(jnp.float32)
    for turn in (turn1, turn2, turn3):
        total = total + turn[...].astype(jnp.float32)
    total = total.astype(jnp.bfloat16)
    rows = near.shape[0]
    near[...] = total[0:rows, :]
    far[...] = total[rows : 2 * rows, :]


def pair_kernel(near, far, out):
    rows = near.shape[0]
    out[0:rows, :] = near[...]
    out[rows : 2 * rows, :] = far[...]


def pack_kernel(turn0, turn1, turn2, turn3, out, sems):
    rows = turn0.shape[0]
    copies = []
    for index, turn in enumerate((turn0, turn1, turn2, turn3)):
        copies.append(pltpu.make_async_copy(turn, out.at[pl.ds(index * rows, rows)], sems.at[index]))
    for copy in copies:
        copy.start()
    for copy in copies:
        copy.wait()


def assemble_kernel(place_ref, near, far, turn0, turn1, turn2, turn3, near_out, far_out, sems):
    rows = turn0.shape[0] // 2

    @pl.when(place_ref[2] == 1)
    def _():
        copies = []
        for index, turn in enumerate((turn0, turn1, turn2, turn3)):
            for half, out in enumerate((near_out, far_out)):
                source = turn.at[pl.ds(half * rows, rows)]
                copies.append(
                    pltpu.make_async_copy(source, out.at[pl.ds(index * rows, rows)], sems.at[2 * index + half])
                )
        for copy in copies:
            copy.start()
        for copy in copies:
            copy.wait()

    @pl.when(place_ref[2] == 0)
    def _():
        copies = [
            pltpu.make_async_copy(near, near_out, sems.at[0]),
            pltpu.make_async_copy(far, far_out, sems.at[1]),
        ]
        for copy in copies:
            copy.start()
        for copy in copies:
            copy.wait()


def fold_kernel(parts, out):
    part = jnp.sum(parts[...].astype(jnp.float32), 0)
    for i in range(out.shape[0]):
        out[i] = part


def spread_kernel(scale, folded, after, spread):
    part = (jnp.sum(folded[...], 0) * scale).astype(jnp.bfloat16)
    for i in range(spread.shape[0]):
        spread[i] = part


def meet_kernel(place_ref, own, near, far, mine, turn1, turn2, turn3):
    rows = mine.shape[0]
    turns = (turn1, turn2, turn3)
    members = len(turns) + 1
    for turn in range(members):
        member = place_ref[1] + turn
        member = jnp.where(member >= members, member - members, member)
        part = pl.ds(pl.multiple_of(member * rows, rows), rows)
        total = own[part, :] + near[part, :].astype(jnp.float32) + far[part, :].astype(jnp.float32)
        if turn == 0:
            mine[...] = total
        else:
            turns[turn - 1][...] = total.astype(jnp.bfloat16)


def last_kernel(mine, turn1, turn2, turn3, near, far, weight, parts, feat, grad):
    total = mine[...]
    for turn in (turn1, turn2, turn3, near, far):
        total = total + turn[...].astype(jnp.float32)
    feat[...] = lax.dot_general(
        total.astype(jnp.bfloat16), weight[...], (((1,), (1,)), ((), ())), preferred_element_type=jnp.float32
    )
    count, depth, _ = parts.shape
    height = grad.shape[0]
    half = height // depth
    for side in range(count // half):
        grad[:, side * TILE : (side + 1) * TILE] = (
            parts[side * half : (side + 1) * half].astype(jnp.float32).reshape(height, TILE)
        )


def params():
    return pltpu.CompilerParams(vmem_limit_bytes=VMEM_LIMIT)


def per_device(features, tile_values, tile_cols, tile_counts, weight, cotangent):
    rows, width = features.shape
    slots = tile_cols.shape[1]
    groups = math.prod(lax.axis_size(axis) for axis in DOM)
    members = lax.axis_size("zl")
    group_rows = rows * members
    x_last, y_last = lax.axis_size("x") - 1, lax.axis_size("y") - 1
    x_at, y_at, core_at = lax.axis_index("x"), lax.axis_index("y"), lax.axis_index("c")
    low_edge = (x_at == 0) & (y_at == 0) & (core_at == 0)
    high_edge = (x_at == x_last) & (y_at == y_last) & (core_at == 1)
    core = jnp.stack([core_at, lax.axis_index("zl"), (low_edge | high_edge).astype(core_at.dtype)]).astype(jnp.int32)
    near, near_across = split_pairs(near_pairs(groups))
    far_inward, far_inward_across = split_pairs(far_pairs(groups, False))
    far_outward, far_outward_across = split_pairs(far_pairs(groups, True))
    edge = edge_devices(groups // 2)
    edge = [2 * k + (0 if k % (groups // 4) == 0 else 1) for k in edge]

    def edge_turned(value, turn):
        pairs = [(d * members + m, d * members + (m + turn) % members) for d in edge for m in range(members)]
        return lax.ppermute(value, ALL, pairs)

    swap = [(0, 1), (1, 0)]
    smem = pl.BlockSpec(memory_space=pltpu.SMEM)
    vmem = pl.BlockSpec(memory_space=pltpu.VMEM)
    anywhere = pl.BlockSpec(memory_space=pl.ANY)
    flops = 2 * 2 * slots * TILE * TILE * width

    near_own = lax.ppermute(features, DOM, near_across)
    far_own = lax.ppermute(features, DOM, far_inward_across)
    turns = [
        lax.ppermute(features, "zl", [(m, (m + turn) % members) for m in range(members)]) for turn in range(1, members)
    ]
    x0 = pl.pallas_call(
        pack_kernel,
        out_shape=jax.ShapeDtypeStruct((group_rows, width), jnp.bfloat16),
        in_specs=[anywhere] * members,
        out_specs=anywhere,
        scratch_shapes=[pltpu.SemaphoreType.DMA((members,))],
        compiler_params=params(),
        name="pack",
    )(features, *turns)
    x1 = lax.ppermute(x0, DOM, near)
    x2 = lax.ppermute(x0, DOM, far_inward)
    edge_pair = pl.pallas_call(
        pair_kernel,
        out_shape=jax.ShapeDtypeStruct((2 * rows, width), jnp.bfloat16),
        in_specs=[vmem, vmem],
        out_specs=vmem,
        compiler_params=params(),
        name="pair",
    )(near_own, far_own)
    edge_turns = [edge_pair] + [edge_turned(edge_pair, turn) for turn in range(1, members)]
    x1, x2 = pl.pallas_call(
        assemble_kernel,
        out_shape=(jax.ShapeDtypeStruct((group_rows, width), jnp.bfloat16),) * 2,
        in_specs=[smem] + [anywhere] * (2 + members),
        out_specs=(anywhere, anywhere),
        scratch_shapes=[pltpu.SemaphoreType.DMA((2 * members,))],
        compiler_params=params(),
        name="assemble",
    )(core, x1, x2, *edge_turns)
    x3 = lax.ppermute(x0, "c", swap)
    x4 = lax.ppermute(x1, "c", swap)

    sent = pl.pallas_call(
        send_kernel,
        out_shape=jax.ShapeDtypeStruct((2 * group_rows, width), jnp.bfloat16),
        in_specs=[smem, smem, smem, vmem, vmem, anywhere],
        out_specs=vmem,
        scratch_shapes=[pltpu.VMEM((2 * group_rows, width), jnp.float32)],
        compiler_params=params(),
        cost_estimate=pl.CostEstimate(flops=flops, bytes_accessed=4 << 20, transcendentals=0),
        name="send",
    )(core, tile_counts, tile_cols, tile_values, cotangent, x0)
    received = lax.ppermute(sent, "c", swap)

    layer_out, local = pl.pallas_call(
        functools.partial(forward_kernel, members),
        out_shape=(
            jax.ShapeDtypeStruct((rows, width), jnp.bfloat16),
            jax.ShapeDtypeStruct((2 * width, TILE), jnp.float32),
        ),
        in_specs=[smem, smem, smem, vmem, vmem, vmem] + [anywhere] * 5,
        out_specs=(vmem, vmem),
        scratch_shapes=[
            pltpu.VMEM((5 * group_rows, width), jnp.bfloat16),
            pltpu.SemaphoreType.DMA((5,)),
        ],
        compiler_params=params(),
        cost_estimate=pl.CostEstimate(flops=flops, bytes_accessed=6 << 20, transcendentals=0),
        name="forward",
    )(core, tile_counts, tile_cols, tile_values, weight, cotangent, x0, x1, x2, x3, x4)

    own, near_sum, far_sum, *chunks = pl.pallas_call(
        keep_kernel,
        out_shape=(
            jax.ShapeDtypeStruct((group_rows, width), jnp.float32),
            jax.ShapeDtypeStruct((group_rows, width), jnp.bfloat16),
            jax.ShapeDtypeStruct((group_rows, width), jnp.bfloat16),
        )
        + (jax.ShapeDtypeStruct((2 * rows, width), jnp.bfloat16),) * members,
        in_specs=[smem, smem, smem, vmem, vmem, vmem, anywhere],
        out_specs=(vmem,) * (3 + members),
        scratch_shapes=[pltpu.VMEM((3 * group_rows, width), jnp.float32)],
        compiler_params=params(),
        cost_estimate=pl.CostEstimate(flops=flops, bytes_accessed=8 << 20, transcendentals=0),
        name="keep",
    )(core, tile_counts, tile_cols, tile_values, cotangent, received, local)
    near_in = lax.ppermute(near_sum, DOM, near)
    far_in = lax.ppermute(far_sum, DOM, far_outward)
    chunk_turns = [edge_turned(chunk, turn) for turn, chunk in enumerate(chunks) if turn > 0]
    near_edge, far_edge = pl.pallas_call(
        cross_kernel,
        out_shape=(jax.ShapeDtypeStruct((rows, width), jnp.bfloat16),) * 2,
        in_specs=[vmem] * members,
        out_specs=(vmem, vmem),
        compiler_params=params(),
        name="cross",
    )(chunks[0], *chunk_turns)
    near_edge = lax.ppermute(near_edge, DOM, near_across)
    far_edge = lax.ppermute(far_edge, DOM, far_outward_across)

    plane = math.prod(lax.axis_size(axis) for axis in PLANE)
    column = math.prod(lax.axis_size(axis) for axis in COLUMN)
    parts = lax.all_to_all(local.reshape(plane, -1, TILE), PLANE, 0, 0)
    part = pl.pallas_call(
        fold_kernel,
        out_shape=jax.ShapeDtypeStruct((column,) + parts.shape[1:], jnp.float32),
        in_specs=[vmem],
        out_specs=vmem,
        compiler_params=params(),
        cost_estimate=pl.CostEstimate(flops=0, bytes_accessed=1 << 20, transcendentals=0),
        name="fold",
    )(parts)
    folded = lax.all_to_all(part, COLUMN, 0, 0)
    mine, *turns = pl.pallas_call(
        meet_kernel,
        out_shape=(jax.ShapeDtypeStruct((rows, width), jnp.float32),)
        + (jax.ShapeDtypeStruct((rows, width), jnp.bfloat16),) * (members - 1),
        in_specs=[smem] + [vmem] * 3,
        out_specs=(vmem,) * members,
        compiler_params=params(),
        name="meet",
    )(core, own, near_in, far_in)
    turns = [
        lax.ppermute(value, "zl", [(m, (m + turn + 1) % members) for m in range(members)])
        for turn, value in enumerate(turns)
    ]
    spread = pl.pallas_call(
        functools.partial(spread_kernel, 1 / math.sqrt(rows * groups * members)),
        out_shape=jax.ShapeDtypeStruct(parts.shape, jnp.bfloat16),
        in_specs=[vmem, anywhere],
        out_specs=vmem,
        compiler_params=params(),
        name="spread",
    )(folded, mine)
    parts = lax.all_to_all(spread, PLANE, 0, 0)
    feat_grad, weight_grad = pl.pallas_call(
        last_kernel,
        out_shape=(
            jax.ShapeDtypeStruct((rows, width), jnp.float32),
            jax.ShapeDtypeStruct(weight.shape, jnp.float32),
        ),
        in_specs=[vmem] * (members + 4),
        out_specs=(vmem, vmem),
        compiler_params=params(),
        name="last",
    )(mine, *turns, near_edge, far_edge, weight, parts)
    return (layer_out, feat_grad, weight_grad)


def solution(mesh):
    split = Mesh(mesh.devices.reshape(2, 8, 8, 2, 4), ALL)
    rows = P(ALL)
    return jax.shard_map(
        per_device,
        mesh=split,
        in_specs=(rows, rows, rows, rows, P(), rows),
        out_specs=(rows, rows, P()),
        check_vma=False,
    )
```

```python
import functools
import math

import jax
import jax.numpy as jnp
from jax import lax
from jax.experimental import pallas as pl
from jax.experimental.pallas import tpu as pltpu
from jax.sharding import Mesh, PartitionSpec as P

TILE = 128
ALL = ("zh", "x", "y", "c", "zl")
DOM = ("zh", "x", "y", "c")
PLANE = ("x", "y")
COLUMN = ("zh", "zl", "c")
VMEM_LIMIT = 24 * 1024 * 1024


def near_pairs(groups):
    pairs = []
    for d in range(groups):
        k, c = d // 2, d % 2
        pairs.append((d, (2 * (k - 1) + 1 if c == 0 else 2 * (k + 1)) % groups))
    return pairs


def far_pairs(groups, outward):
    pairs = []
    for d in range(groups):
        step = 2 if (d % 2 == 1) == outward else -2
        pairs.append((d, (d + step) % groups))
    return pairs


def split_pairs(pairs):
    part = len(pairs) // 2
    inside = [(a, b) for a, b in pairs if a // part == b // part]
    across = [(a, b) for a, b in pairs if a // part != b // part]
    return inside, across


def edge_devices(groups):
    part = groups // 2
    return [d for d in range(groups) if d % part in (0, part - 1)]


def tile_of(col, core, per_group):
    band = col // per_group
    band = jnp.where(core == 0, 4 - band, band)
    place = jnp.where(band >= 2, band - 2, 4 - band)
    return place * per_group + col % per_group


def forward_kernel(place_ref, counts, cols, tiles, weight, cotangent, x0, x1, x2, x3, x4, out, local, band, sems):
    sources = (x0, x1, x2, x3, x4)
    rows = x0.shape[0]
    per_group = rows // TILE
    copies = []
    for index, source in enumerate(sources):
        copy = pltpu.make_async_copy(source, band.at[pl.ds(index * rows, rows)], sems.at[index])
        copy.start()
        copies.append(copy)
    for copy in copies:
        copy.wait()
    core = place_ref[0]
    slots = tiles.shape[1]
    sums = []
    for t in range(tiles.shape[0]):
        count = counts[t]
        total = jnp.zeros((TILE, x0.shape[1]), jnp.float32)
        for s in range(0, slots, 2):
            left, right = [], []
            for one in (s, s + 1):
                start = pl.multiple_of(tile_of(cols[t, one], core, per_group) * TILE, TILE)
                value = tiles[t, one]
                left.append(jnp.where(one < count, value, jnp.zeros_like(value)))
                right.append(band[pl.ds(start, TILE), :])
            total = total + jnp.dot(
                jnp.concatenate(left, 1), jnp.concatenate(right, 0), preferred_element_type=jnp.float32
            )
        sums.append(total.astype(jnp.bfloat16))
    aggregated = jnp.concatenate(sums, 0)
    out[...] = jnp.dot(aggregated, weight[...], preferred_element_type=jnp.float32).astype(jnp.bfloat16)
    grad = lax.dot_general(
        aggregated, cotangent[...], (((0,), (0,)), ((), ())), preferred_element_type=jnp.float32
    )
    height = grad.shape[0]
    local[0:height, :] = grad[:, 0:TILE]
    local[height : 2 * height, :] = grad[:, TILE : 2 * TILE]


def scatter_tiles(core, counts, cols, tiles, cotangent, total, least, most, per_group):
    for t in range(tiles.shape[0]):
        grads = cotangent[t * TILE : (t + 1) * TILE, :]

        def step(s, carry):
            place = tile_of(cols[t, s], core, per_group)

            @pl.when((place >= least) & (place < most))
            def _():
                start = pl.multiple_of((place - least) * TILE, TILE)
                total[pl.ds(start, TILE), :] += lax.dot_general(
                    tiles[t, s], grads, (((0,), (0,)), ((), ())), preferred_element_type=jnp.float32
                )

            return carry

        lax.fori_loop(0, counts[t], step, 0)


def send_kernel(place_ref, counts, cols, tiles, cotangent, after, out, total):
    per_group = out.shape[0] // TILE // 2
    total[...] = jnp.zeros_like(total)
    scatter_tiles(place_ref[0], counts, cols, tiles, cotangent, total, 3 * per_group, 5 * per_group, per_group)
    out[...] = total[...].astype(jnp.bfloat16)


def keep_kernel(
    place_ref, counts, cols, tiles, cotangent, received, after, own, near, far, chunk0, chunk1, chunk2, chunk3, total
):
    rows = own.shape[0]
    per_group = rows // TILE
    total[0 : 2 * rows, :] = received[...].astype(jnp.float32)
    total[2 * rows : 3 * rows, :] = jnp.zeros_like(total[2 * rows : 3 * rows, :])
    scatter_tiles(place_ref[0], counts, cols, tiles, cotangent, total, 0, 3 * per_group, per_group)
    own[...] = total[0:rows, :]
    near[...] = total[rows : 2 * rows, :].astype(jnp.bfloat16)
    far[...] = total[2 * rows : 3 * rows, :].astype(jnp.bfloat16)
    chunks = (chunk0, chunk1, chunk2, chunk3)
    size = chunk0.shape[0] // 2

    @pl.when(place_ref[2] == 1)
    def _():
        for turn, chunk in enumerate(chunks):
            member = place_ref[1] + turn
            member = jnp.where(member >= len(chunks), member - len(chunks), member)
            for index in (1, 2):
                start = pl.multiple_of(index * rows + member * size, size)
                chunk[(index - 1) * size : index * size, :] = total[pl.ds(start, size), :].astype(jnp.bfloat16)

    @pl.when(place_ref[2] == 0)
    def _():
        for chunk in chunks:
            chunk[...] = jnp.zeros_like(chunk)


def cross_kernel(chunk, turn1, turn2, turn3, after, near, far):
    total = chunk[...].astype(jnp.float32)
    for turn in (turn1, turn2, turn3):
        total = total + turn[...].astype(jnp.float32)
    total = total.astype(jnp.bfloat16)
    rows = near.shape[0]
    near[...] = total[0:rows, :]
    far[...] = total[rows : 2 * rows, :]


def fold_kernel(parts, out):
    part = jnp.sum(parts[...].astype(jnp.float32), 0)
    for i in range(out.shape[0]):
        out[i] = part


def spread_kernel(scale, folded, *refs):
    spread = refs[-1]
    part = (jnp.sum(folded[...], 0) * scale).astype(jnp.bfloat16)
    for i in range(spread.shape[0]):
        spread[i] = part


def meet_kernel(place_ref, own, near, far, mine, turn1, turn2, turn3):
    rows = mine.shape[0]
    turns = (turn1, turn2, turn3)
    members = len(turns) + 1
    for turn in range(members):
        member = place_ref[1] + turn
        member = jnp.where(member >= members, member - members, member)
        part = pl.ds(pl.multiple_of(member * rows, rows), rows)
        total = own[part, :] + near[part, :].astype(jnp.float32) + far[part, :].astype(jnp.float32)
        if turn == 0:
            mine[...] = total
        else:
            turns[turn - 1][...] = total.astype(jnp.bfloat16)


def last_kernel(mine, turn1, turn2, turn3, near, far, weight, parts, feat, grad):
    total = mine[...]
    for turn in (turn1, turn2, turn3, near, far):
        total = total + turn[...].astype(jnp.float32)
    feat[...] = lax.dot_general(
        total.astype(jnp.bfloat16), weight[...], (((1,), (1,)), ((), ())), preferred_element_type=jnp.float32
    )
    count, depth, _ = parts.shape
    height = grad.shape[0]
    half = height // depth
    for side in range(count // half):
        grad[:, side * TILE : (side + 1) * TILE] = (
            parts[side * half : (side + 1) * half].astype(jnp.float32).reshape(height, TILE)
        )


def params():
    return pltpu.CompilerParams(vmem_limit_bytes=VMEM_LIMIT)


def per_device(features, tile_values, tile_cols, tile_counts, weight, cotangent):
    rows, width = features.shape
    slots = tile_cols.shape[1]
    groups = math.prod(lax.axis_size(axis) for axis in DOM)
    members = lax.axis_size("zl")
    group_rows = rows * members
    x_last, y_last = lax.axis_size("x") - 1, lax.axis_size("y") - 1
    x_at, y_at, core_at = lax.axis_index("x"), lax.axis_index("y"), lax.axis_index("c")
    low_edge = (x_at == 0) & (y_at == 0) & (core_at == 0)
    high_edge = (x_at == x_last) & (y_at == y_last) & (core_at == 1)
    core = jnp.stack([core_at, lax.axis_index("zl"), (low_edge | high_edge).astype(core_at.dtype)]).astype(jnp.int32)
    near, near_across = split_pairs(near_pairs(groups))
    far_inward = far_pairs(groups, False)
    far_outward, far_outward_across = split_pairs(far_pairs(groups, True))
    edge = edge_devices(groups // 2)
    edge = [2 * k + (0 if k % (groups // 4) == 0 else 1) for k in edge]

    def edge_turned(value, turn):
        pairs = [(d * members + m, d * members + (m + turn) % members) for d in edge for m in range(members)]
        return lax.ppermute(value, ALL, pairs)

    swap = [(0, 1), (1, 0)]
    smem = pl.BlockSpec(memory_space=pltpu.SMEM)
    vmem = pl.BlockSpec(memory_space=pltpu.VMEM)
    anywhere = pl.BlockSpec(memory_space=pl.ANY)
    flops = 2 * 2 * slots * TILE * TILE * width

    x0 = lax.all_gather(features, "zl", axis=0, tiled=True)
    x1 = lax.ppermute(x0, DOM, near + near_across)
    x2 = lax.ppermute(x0, DOM, far_inward)
    x3 = lax.ppermute(x0, "c", swap)
    x4 = lax.ppermute(x1, "c", swap)

    sent = pl.pallas_call(
        send_kernel,
        out_shape=jax.ShapeDtypeStruct((2 * group_rows, width), jnp.bfloat16),
        in_specs=[smem, smem, smem, vmem, vmem, anywhere],
        out_specs=vmem,
        scratch_shapes=[pltpu.VMEM((2 * group_rows, width), jnp.float32)],
        compiler_params=params(),
        cost_estimate=pl.CostEstimate(flops=flops, bytes_accessed=4 << 20, transcendentals=0),
        name="send",
    )(core, tile_counts, tile_cols, tile_values, cotangent, x0)
    received = lax.ppermute(sent, "c", swap)

    layer_out, local = pl.pallas_call(
        forward_kernel,
        out_shape=(
            jax.ShapeDtypeStruct((rows, width), jnp.bfloat16),
            jax.ShapeDtypeStruct((2 * width, TILE), jnp.float32),
        ),
        in_specs=[smem, smem, smem, vmem, vmem, vmem] + [anywhere] * 5,
        out_specs=(vmem, vmem),
        scratch_shapes=[
            pltpu.VMEM((5 * group_rows, width), jnp.bfloat16),
            pltpu.SemaphoreType.DMA((5,)),
        ],
        compiler_params=params(),
        cost_estimate=pl.CostEstimate(flops=flops, bytes_accessed=6 << 20, transcendentals=0),
        name="forward",
    )(core, tile_counts, tile_cols, tile_values, weight, cotangent, x0, x1, x2, x3, x4)

    own, near_sum, far_sum, *chunks = pl.pallas_call(
        keep_kernel,
        out_shape=(
            jax.ShapeDtypeStruct((group_rows, width), jnp.float32),
            jax.ShapeDtypeStruct((group_rows, width), jnp.bfloat16),
            jax.ShapeDtypeStruct((group_rows, width), jnp.bfloat16),
        )
        + (jax.ShapeDtypeStruct((2 * rows, width), jnp.bfloat16),) * members,
        in_specs=[smem, smem, smem, vmem, vmem, vmem, anywhere],
        out_specs=(vmem,) * (3 + members),
        scratch_shapes=[pltpu.VMEM((3 * group_rows, width), jnp.float32)],
        compiler_params=params(),
        cost_estimate=pl.CostEstimate(flops=flops, bytes_accessed=8 << 20, transcendentals=0),
        name="keep",
    )(core, tile_counts, tile_cols, tile_values, cotangent, received, x1)
    near_in = lax.ppermute(near_sum, DOM, near)
    far_in = lax.ppermute(far_sum, DOM, far_outward)
    chunk_turns = [edge_turned(chunk, turn) for turn, chunk in enumerate(chunks) if turn > 0]

    plane = math.prod(lax.axis_size(axis) for axis in PLANE)
    column = math.prod(lax.axis_size(axis) for axis in COLUMN)
    parts = lax.all_to_all(local.reshape(plane, -1, TILE), PLANE, 0, 0)
    part = pl.pallas_call(
        fold_kernel,
        out_shape=jax.ShapeDtypeStruct((column,) + parts.shape[1:], jnp.float32),
        in_specs=[vmem],
        out_specs=vmem,
        compiler_params=params(),
        cost_estimate=pl.CostEstimate(flops=0, bytes_accessed=1 << 20, transcendentals=0),
        name="fold",
    )(parts)
    folded = lax.all_to_all(part, COLUMN, 0, 0)
    near_edge, far_edge = pl.pallas_call(
        cross_kernel,
        out_shape=(jax.ShapeDtypeStruct((rows, width), jnp.bfloat16),) * 2,
        in_specs=[vmem] * members + [anywhere],
        out_specs=(vmem, vmem),
        compiler_params=params(),
        name="cross",
    )(chunks[0], *chunk_turns, part)
    near_edge = lax.ppermute(near_edge, DOM, near_across)
    far_edge = lax.ppermute(far_edge, DOM, far_outward_across)
    mine, *turns = pl.pallas_call(
        meet_kernel,
        out_shape=(jax.ShapeDtypeStruct((rows, width), jnp.float32),)
        + (jax.ShapeDtypeStruct((rows, width), jnp.bfloat16),) * (members - 1),
        in_specs=[smem] + [vmem] * 3,
        out_specs=(vmem,) * members,
        compiler_params=params(),
        name="meet",
    )(core, own, near_in, far_in)
    turns = [
        lax.ppermute(value, "zl", [(m, (m + turn + 1) % members) for m in range(members)])
        for turn, value in enumerate(turns)
    ]
    spread = pl.pallas_call(
        functools.partial(spread_kernel, 1 / math.sqrt(rows * groups * members)),
        out_shape=jax.ShapeDtypeStruct(parts.shape, jnp.bfloat16),
        in_specs=[vmem] + [anywhere] * 3,
        out_specs=vmem,
        compiler_params=params(),
        name="spread",
    )(folded, *turns)
    parts = lax.all_to_all(spread, PLANE, 0, 0)
    feat_grad, weight_grad = pl.pallas_call(
        last_kernel,
        out_shape=(
            jax.ShapeDtypeStruct((rows, width), jnp.float32),
            jax.ShapeDtypeStruct(weight.shape, jnp.float32),
        ),
        in_specs=[vmem] * (members + 4),
        out_specs=(vmem, vmem),
        compiler_params=params(),
        name="last",
    )(mine, *turns, near_edge, far_edge, weight, parts)
    return (layer_out, feat_grad, weight_grad)


def solution(mesh):
    split = Mesh(mesh.devices.reshape(2, 8, 8, 2, 4), ALL)
    rows = P(ALL)
    return jax.shard_map(
        per_device,
        mesh=split,
        in_specs=(rows, rows, rows, rows, P(), rows),
        out_specs=(rows, rows, P()),
        check_vma=False,
    )
```

```python
import functools
import math

import jax
import jax.numpy as jnp
from jax import lax
from jax.experimental import pallas as pl
from jax.experimental.pallas import tpu as pltpu
from jax.sharding import Mesh, PartitionSpec as P

TILE = 128
ALL = ("zh", "x", "y", "c", "zl")
DOM = ("zh", "x", "y", "c")
PLANE = ("x", "y")
COLUMN = ("zh", "zl", "c")
VMEM_LIMIT = 24 * 1024 * 1024


def near_pairs(groups, outward):
    pairs = []
    for d in range(groups):
        step = 2 if (d % 2 == 1) == outward else -2
        pairs.append((d, (d + step) % groups))
    return pairs


def far_pairs(groups):
    return [(d, (d + (3 if d % 2 == 0 else -3)) % groups) for d in range(groups)]


def tile_of(col, core, per_group):
    band = col // per_group
    band = jnp.where(core == 0, band, 4 - band)
    place = jnp.where(band >= 3, jnp.where(band == 3, 3, 1), jnp.where(band == 2, 0, 5 - band))
    return place * per_group + col % per_group


def forward_kernel(place_ref, counts, cols, tiles, weight, cotangent, x0, x1, x3, x4, x5, out, local, band, sems):
    sources = ((0, x0), (1, x1), (3, x3), (4, x4), (5, x5))
    rows = x0.shape[0]
    per_group = rows // TILE
    copies = []
    for index, (place, source) in enumerate(sources):
        copy = pltpu.make_async_copy(source, band.at[pl.ds(place * rows, rows)], sems.at[index])
        copy.start()
        copies.append(copy)
    for copy in copies:
        copy.wait()
    core = place_ref[0]
    slots = tiles.shape[1]
    sums = []
    for t in range(tiles.shape[0]):
        count = counts[t]
        total = jnp.zeros((TILE, x0.shape[1]), jnp.float32)
        for s in range(0, slots, 2):
            left, right = [], []
            for one in (s, s + 1):
                start = pl.multiple_of(tile_of(cols[t, one], core, per_group) * TILE, TILE)
                value = tiles[t, one]
                left.append(jnp.where(one < count, value, jnp.zeros_like(value)))
                right.append(band[pl.ds(start, TILE), :])
            total = total + jnp.dot(
                jnp.concatenate(left, 1), jnp.concatenate(right, 0), preferred_element_type=jnp.float32
            )
        sums.append(total.astype(jnp.bfloat16))
    aggregated = jnp.concatenate(sums, 0)
    out[...] = jnp.dot(aggregated, weight[...], preferred_element_type=jnp.float32).astype(jnp.bfloat16)
    grad = lax.dot_general(
        aggregated, cotangent[...], (((0,), (0,)), ((), ())), preferred_element_type=jnp.float32
    )
    height = grad.shape[0]
    local[0:height, :] = grad[:, 0:TILE]
    local[height : 2 * height, :] = grad[:, TILE : 2 * TILE]


def scatter_tiles(core, counts, cols, tiles, cotangent, total, least, most, per_group):
    for t in range(tiles.shape[0]):
        grads = cotangent[t * TILE : (t + 1) * TILE, :]

        def step(s, carry):
            place = tile_of(cols[t, s], core, per_group)

            @pl.when((place >= least) & (place < most))
            def _():
                start = pl.multiple_of((place - least) * TILE, TILE)
                total[pl.ds(start, TILE), :] += lax.dot_general(
                    tiles[t, s], grads, (((0,), (0,)), ((), ())), preferred_element_type=jnp.float32
                )

            return carry

        lax.fori_loop(0, counts[t], step, 0)


def send_kernel(place_ref, counts, cols, tiles, cotangent, after, out, total):
    per_group = out.shape[0] // TILE // 3
    total[...] = jnp.zeros_like(total)
    scatter_tiles(place_ref[0], counts, cols, tiles, cotangent, total, 3 * per_group, 6 * per_group, per_group)
    out[...] = total[...].astype(jnp.bfloat16)


def keep_kernel(place_ref, counts, cols, tiles, cotangent, received, after, own, near, far, total):
    rows = own.shape[0]
    per_group = rows // TILE
    total[...] = received[0 : 2 * rows, :].astype(jnp.float32)
    scatter_tiles(place_ref[0], counts, cols, tiles, cotangent, total, 0, 2 * per_group, per_group)
    own[...] = total[0:rows, :]
    near[...] = total[rows : 2 * rows, :].astype(jnp.bfloat16)
    far[...] = received[2 * rows : 3 * rows, :]


def fold_kernel(parts, out):
    part = jnp.sum(parts[...].astype(jnp.float32), 0)
    for i in range(out.shape[0]):
        out[i] = part


def spread_kernel(scale, folded, spread):
    part = (jnp.sum(folded[...], 0) * scale).astype(jnp.bfloat16)
    for i in range(spread.shape[0]):
        spread[i] = part


def meet_kernel(place_ref, own, near, far, mine, turn1, turn2, turn3):
    rows = mine.shape[0]
    turns = (turn1, turn2, turn3)
    members = len(turns) + 1
    for turn in range(members):
        member = place_ref[1] + turn
        member = jnp.where(member >= members, member - members, member)
        part = pl.ds(pl.multiple_of(member * rows, rows), rows)
        total = own[part, :] + near[part, :].astype(jnp.float32) + far[part, :].astype(jnp.float32)
        if turn == 0:
            mine[...] = total
        else:
            turns[turn - 1][...] = total.astype(jnp.bfloat16)


def last_kernel(mine, turn1, turn2, turn3, weight, parts, feat, grad):
    total = mine[...]
    for turn in (turn1, turn2, turn3):
        total = total + turn[...].astype(jnp.float32)
    feat[...] = lax.dot_general(
        total.astype(jnp.bfloat16), weight[...], (((1,), (1,)), ((), ())), preferred_element_type=jnp.float32
    )
    count, depth, _ = parts.shape
    height = grad.shape[0]
    half = height // depth
    for side in range(count // half):
        grad[:, side * TILE : (side + 1) * TILE] = (
            parts[side * half : (side + 1) * half].astype(jnp.float32).reshape(height, TILE)
        )


def params():
    return pltpu.CompilerParams(vmem_limit_bytes=VMEM_LIMIT)


def per_device(features, tile_values, tile_cols, tile_counts, weight, cotangent):
    rows, width = features.shape
    slots = tile_cols.shape[1]
    groups = math.prod(lax.axis_size(axis) for axis in DOM)
    members = lax.axis_size("zl")
    group_rows = rows * members
    core = jnp.stack([lax.axis_index("c"), lax.axis_index("zl")]).astype(jnp.int32)
    swap = [(0, 1), (1, 0)]
    smem = pl.BlockSpec(memory_space=pltpu.SMEM)
    vmem = pl.BlockSpec(memory_space=pltpu.VMEM)
    anywhere = pl.BlockSpec(memory_space=pl.ANY)
    flops = 2 * 2 * slots * TILE * TILE * width

    x0 = lax.all_gather(features, "zl", axis=0, tiled=True)
    x1 = lax.ppermute(x0, DOM, near_pairs(groups, True))
    x2 = lax.ppermute(x0, DOM, far_pairs(groups))
    x3 = lax.ppermute(x0, "c", swap)
    x4 = lax.ppermute(x1, "c", swap)
    x5 = lax.ppermute(x2, "c", swap)

    layer_out, local = pl.pallas_call(
        forward_kernel,
        out_shape=(
            jax.ShapeDtypeStruct((rows, width), jnp.bfloat16),
            jax.ShapeDtypeStruct((2 * width, TILE), jnp.float32),
        ),
        in_specs=[smem, smem, smem, vmem, vmem, vmem] + [anywhere] * 5,
        out_specs=(vmem, vmem),
        scratch_shapes=[
            pltpu.VMEM((6 * group_rows, width), jnp.bfloat16),
            pltpu.SemaphoreType.DMA((5,)),
        ],
        compiler_params=params(),
        cost_estimate=pl.CostEstimate(flops=flops, bytes_accessed=6 << 20, transcendentals=0),
        name="forward",
    )(core, tile_counts, tile_cols, tile_values, weight, cotangent, x0, x1, x3, x4, x5)

    sent = pl.pallas_call(
        send_kernel,
        out_shape=jax.ShapeDtypeStruct((3 * group_rows, width), jnp.bfloat16),
        in_specs=[smem, smem, smem, vmem, vmem, anywhere],
        out_specs=vmem,
        scratch_shapes=[pltpu.VMEM((3 * group_rows, width), jnp.float32)],
        compiler_params=params(),
        cost_estimate=pl.CostEstimate(flops=flops, bytes_accessed=4 << 20, transcendentals=0),
        name="send",
    )(core, tile_counts, tile_cols, tile_values, cotangent, local)
    received = lax.ppermute(sent, "c", swap)

    own, near_sum, far_sum = pl.pallas_call(
        keep_kernel,
        out_shape=(
            jax.ShapeDtypeStruct((group_rows, width), jnp.float32),
            jax.ShapeDtypeStruct((group_rows, width), jnp.bfloat16),
            jax.ShapeDtypeStruct((group_rows, width), jnp.bfloat16),
        ),
        in_specs=[smem, smem, smem, vmem, vmem, vmem, anywhere],
        out_specs=(vmem, vmem, vmem),
        scratch_shapes=[pltpu.VMEM((2 * group_rows, width), jnp.float32)],
        compiler_params=params(),
        cost_estimate=pl.CostEstimate(flops=flops, bytes_accessed=8 << 20, transcendentals=0),
        name="keep",
    )(core, tile_counts, tile_cols, tile_values, cotangent, received, local)
    near_in = lax.ppermute(near_sum, DOM, near_pairs(groups, False))
    far_in = lax.ppermute(far_sum, DOM, far_pairs(groups))

    plane = math.prod(lax.axis_size(axis) for axis in PLANE)
    column = math.prod(lax.axis_size(axis) for axis in COLUMN)
    parts = lax.all_to_all(local.reshape(plane, -1, TILE), PLANE, 0, 0)
    part = pl.pallas_call(
        fold_kernel,
        out_shape=jax.ShapeDtypeStruct((column,) + parts.shape[1:], jnp.float32),
        in_specs=[vmem],
        out_specs=vmem,
        compiler_params=params(),
        cost_estimate=pl.CostEstimate(flops=0, bytes_accessed=1 << 20, transcendentals=0),
        name="fold",
    )(parts)
    folded = lax.all_to_all(part, COLUMN, 0, 0)
    mine, *turns = pl.pallas_call(
        meet_kernel,
        out_shape=(jax.ShapeDtypeStruct((rows, width), jnp.float32),)
        + (jax.ShapeDtypeStruct((rows, width), jnp.bfloat16),) * (members - 1),
        in_specs=[smem] + [vmem] * 3,
        out_specs=(vmem,) * members,
        compiler_params=params(),
        name="meet",
    )(core, own, near_in, far_in)
    turns = [
        lax.ppermute(value, "zl", [(m, (m + turn + 1) % members) for m in range(members)])
        for turn, value in enumerate(turns)
    ]
    spread = pl.pallas_call(
        functools.partial(spread_kernel, 1 / math.sqrt(rows * groups * members)),
        out_shape=jax.ShapeDtypeStruct(parts.shape, jnp.bfloat16),
        in_specs=[vmem],
        out_specs=vmem,
        compiler_params=params(),
        name="spread",
    )(folded)
    parts = lax.all_to_all(spread, PLANE, 0, 0)
    feat_grad, weight_grad = pl.pallas_call(
        last_kernel,
        out_shape=(
            jax.ShapeDtypeStruct((rows, width), jnp.float32),
            jax.ShapeDtypeStruct(weight.shape, jnp.float32),
        ),
        in_specs=[vmem] * (members + 2),
        out_specs=(vmem, vmem),
        compiler_params=params(),
        name="last",
    )(mine, *turns, weight, parts)
    return (layer_out, feat_grad, weight_grad)


def solution(mesh):
    split = Mesh(mesh.devices.reshape(2, 8, 8, 2, 4), ALL)
    rows = P(ALL)
    return jax.shard_map(
        per_device,
        mesh=split,
        in_specs=(rows, rows, rows, rows, P(), rows),
        out_specs=(rows, rows, P()),
        check_vma=False,
    )
```

```python
import functools
import math

import jax
import jax.numpy as jnp
from jax import lax
from jax.experimental import pallas as pl
from jax.experimental.pallas import tpu as pltpu
from jax.sharding import Mesh, PartitionSpec as P

TILE = 128
ALL = ("zh", "x", "y", "c", "zl")
DOM = ("zh", "x", "y", "c")
PLANE = ("x", "y")
COLUMN = ("zh", "zl", "c")
VMEM_LIMIT = 24 * 1024 * 1024


def near_pairs(groups):
    pairs = []
    for d in range(groups):
        k, c = d // 2, d % 2
        pairs.append((d, (2 * (k - 1) + 1 if c == 0 else 2 * (k + 1)) % groups))
    return pairs


def far_pairs(groups, outward):
    pairs = []
    for d in range(groups):
        step = 2 if (d % 2 == 1) == outward else -2
        pairs.append((d, (d + step) % groups))
    return pairs


def tile_of(col, core, per_group):
    band = col // per_group
    band = jnp.where(core == 0, 4 - band, band)
    place = jnp.where(band >= 2, band - 2, 4 - band)
    return place * per_group + col % per_group


def forward_kernel(place_ref, counts, cols, tiles, weight, cotangent, x0, x1, x2, x3, x4, out, local, band, sems):
    sources = (x0, x1, x2, x3, x4)
    rows = x0.shape[0]
    per_group = rows // TILE
    copies = []
    for index, source in enumerate(sources):
        copy = pltpu.make_async_copy(source, band.at[pl.ds(index * rows, rows)], sems.at[index])
        copy.start()
        copies.append(copy)
    for copy in copies:
        copy.wait()
    core = place_ref[0]
    slots = tiles.shape[1]
    sums = []
    for t in range(tiles.shape[0]):
        count = counts[t]
        total = jnp.zeros((TILE, x0.shape[1]), jnp.float32)
        for s in range(0, slots, 2):
            left, right = [], []
            for one in (s, s + 1):
                start = pl.multiple_of(tile_of(cols[t, one], core, per_group) * TILE, TILE)
                value = tiles[t, one]
                left.append(jnp.where(one < count, value, jnp.zeros_like(value)))
                right.append(band[pl.ds(start, TILE), :])
            total = total + jnp.dot(
                jnp.concatenate(left, 1), jnp.concatenate(right, 0), preferred_element_type=jnp.float32
            )
        sums.append(total.astype(jnp.bfloat16))
    aggregated = jnp.concatenate(sums, 0)
    out[...] = jnp.dot(aggregated, weight[...], preferred_element_type=jnp.float32).astype(jnp.bfloat16)
    grad = lax.dot_general(
        aggregated, cotangent[...], (((0,), (0,)), ((), ())), preferred_element_type=jnp.float32
    )
    height = grad.shape[0]
    local[0:height, :] = grad[:, 0:TILE]
    local[height : 2 * height, :] = grad[:, TILE : 2 * TILE]


def scatter_tiles(core, counts, cols, tiles, cotangent, total, least, most, per_group):
    for t in range(tiles.shape[0]):
        grads = cotangent[t * TILE : (t + 1) * TILE, :]

        def step(s, carry):
            place = tile_of(cols[t, s], core, per_group)

            @pl.when((place >= least) & (place < most))
            def _():
                start = pl.multiple_of((place - least) * TILE, TILE)
                total[pl.ds(start, TILE), :] += lax.dot_general(
                    tiles[t, s], grads, (((0,), (0,)), ((), ())), preferred_element_type=jnp.float32
                )

            return carry

        lax.fori_loop(0, counts[t], step, 0)


def send_kernel(place_ref, counts, cols, tiles, cotangent, after, out, total):
    per_group = out.shape[0] // TILE // 2
    total[...] = jnp.zeros_like(total)
    scatter_tiles(place_ref[0], counts, cols, tiles, cotangent, total, 3 * per_group, 5 * per_group, per_group)
    out[...] = total[...].astype(jnp.bfloat16)


def keep_kernel(place_ref, counts, cols, tiles, cotangent, received, after, own, near, far, total):
    rows = own.shape[0]
    per_group = rows // TILE
    total[0 : 2 * rows, :] = received[...].astype(jnp.float32)
    total[2 * rows : 3 * rows, :] = jnp.zeros_like(total[2 * rows : 3 * rows, :])
    scatter_tiles(place_ref[0], counts, cols, tiles, cotangent, total, 0, 3 * per_group, per_group)
    own[...] = total[0:rows, :]
    near[...] = total[rows : 2 * rows, :].astype(jnp.bfloat16)
    far[...] = total[2 * rows : 3 * rows, :].astype(jnp.bfloat16)


def fold_kernel(parts, out):
    part = jnp.sum(parts[...].astype(jnp.float32), 0)
    for i in range(out.shape[0]):
        out[i] = part


def spread_kernel(scale, folded, *refs):
    spread = refs[-1]
    part = (jnp.sum(folded[...], 0) * scale).astype(jnp.bfloat16)
    for i in range(spread.shape[0]):
        spread[i] = part


def meet_kernel(place_ref, own, near, far, mine, turn1, turn2, turn3):
    rows = mine.shape[0]
    turns = (turn1, turn2, turn3)
    members = len(turns) + 1
    for turn in range(members):
        member = place_ref[1] + turn
        member = jnp.where(member >= members, member - members, member)
        part = pl.ds(pl.multiple_of(member * rows, rows), rows)
        total = own[part, :] + near[part, :].astype(jnp.float32) + far[part, :].astype(jnp.float32)
        if turn == 0:
            mine[...] = total
        else:
            turns[turn - 1][...] = total.astype(jnp.bfloat16)


def last_kernel(mine, turn1, turn2, turn3, weight, parts, feat, grad):
    total = mine[...]
    for turn in (turn1, turn2, turn3):
        total = total + turn[...].astype(jnp.float32)
    feat[...] = lax.dot_general(
        total.astype(jnp.bfloat16), weight[...], (((1,), (1,)), ((), ())), preferred_element_type=jnp.float32
    )
    count, depth, _ = parts.shape
    height = grad.shape[0]
    half = height // depth
    for side in range(count // half):
        grad[:, side * TILE : (side + 1) * TILE] = (
            parts[side * half : (side + 1) * half].astype(jnp.float32).reshape(height, TILE)
        )


def params():
    return pltpu.CompilerParams(vmem_limit_bytes=VMEM_LIMIT)


def per_device(features, tile_values, tile_cols, tile_counts, weight, cotangent):
    rows, width = features.shape
    slots = tile_cols.shape[1]
    groups = math.prod(lax.axis_size(axis) for axis in DOM)
    members = lax.axis_size("zl")
    group_rows = rows * members
    core = jnp.stack([lax.axis_index("c"), lax.axis_index("zl")]).astype(jnp.int32)
    near = near_pairs(groups)
    swap = [(0, 1), (1, 0)]
    smem = pl.BlockSpec(memory_space=pltpu.SMEM)
    vmem = pl.BlockSpec(memory_space=pltpu.VMEM)
    anywhere = pl.BlockSpec(memory_space=pl.ANY)
    flops = 2 * 2 * slots * TILE * TILE * width

    x0 = lax.all_gather(features, "zl", axis=0, tiled=True)
    x1 = lax.ppermute(x0, DOM, near)
    x2 = lax.ppermute(x0, DOM, far_pairs(groups, False))
    x3 = lax.ppermute(x0, "c", swap)
    x4 = lax.ppermute(x1, "c", swap)

    sent = pl.pallas_call(
        send_kernel,
        out_shape=jax.ShapeDtypeStruct((2 * group_rows, width), jnp.bfloat16),
        in_specs=[smem, smem, smem, vmem, vmem, anywhere],
        out_specs=vmem,
        scratch_shapes=[pltpu.VMEM((2 * group_rows, width), jnp.float32)],
        compiler_params=params(),
        cost_estimate=pl.CostEstimate(flops=flops, bytes_accessed=4 << 20, transcendentals=0),
        name="send",
    )(core, tile_counts, tile_cols, tile_values, cotangent, x0)
    received = lax.ppermute(sent, "c", swap)

    layer_out, local = pl.pallas_call(
        forward_kernel,
        out_shape=(
            jax.ShapeDtypeStruct((rows, width), jnp.bfloat16),
            jax.ShapeDtypeStruct((2 * width, TILE), jnp.float32),
        ),
        in_specs=[smem, smem, smem, vmem, vmem, vmem] + [anywhere] * 5,
        out_specs=(vmem, vmem),
        scratch_shapes=[
            pltpu.VMEM((5 * group_rows, width), jnp.bfloat16),
            pltpu.SemaphoreType.DMA((5,)),
        ],
        compiler_params=params(),
        cost_estimate=pl.CostEstimate(flops=flops, bytes_accessed=6 << 20, transcendentals=0),
        name="forward",
    )(core, tile_counts, tile_cols, tile_values, weight, cotangent, x0, x1, x2, x3, x4)

    own, near_sum, far_sum = pl.pallas_call(
        keep_kernel,
        out_shape=(
            jax.ShapeDtypeStruct((group_rows, width), jnp.float32),
            jax.ShapeDtypeStruct((group_rows, width), jnp.bfloat16),
            jax.ShapeDtypeStruct((group_rows, width), jnp.bfloat16),
        ),
        in_specs=[smem, smem, smem, vmem, vmem, vmem, anywhere],
        out_specs=(vmem, vmem, vmem),
        scratch_shapes=[pltpu.VMEM((3 * group_rows, width), jnp.float32)],
        compiler_params=params(),
        cost_estimate=pl.CostEstimate(flops=flops, bytes_accessed=8 << 20, transcendentals=0),
        name="keep",
    )(core, tile_counts, tile_cols, tile_values, cotangent, received, local)
    near_in = lax.ppermute(near_sum, DOM, near)
    far_in = lax.ppermute(far_sum, DOM, far_pairs(groups, True))

    plane = math.prod(lax.axis_size(axis) for axis in PLANE)
    column = math.prod(lax.axis_size(axis) for axis in COLUMN)
    parts = lax.all_to_all(local.reshape(plane, -1, TILE), PLANE, 0, 0)
    part = pl.pallas_call(
        fold_kernel,
        out_shape=jax.ShapeDtypeStruct((column,) + parts.shape[1:], jnp.float32),
        in_specs=[vmem],
        out_specs=vmem,
        compiler_params=params(),
        cost_estimate=pl.CostEstimate(flops=0, bytes_accessed=1 << 20, transcendentals=0),
        name="fold",
    )(parts)
    folded = lax.all_to_all(part, COLUMN, 0, 0)
    mine, *turns = pl.pallas_call(
        meet_kernel,
        out_shape=(jax.ShapeDtypeStruct((rows, width), jnp.float32),)
        + (jax.ShapeDtypeStruct((rows, width), jnp.bfloat16),) * (members - 1),
        in_specs=[smem] + [vmem] * 3,
        out_specs=(vmem,) * members,
        compiler_params=params(),
        name="meet",
    )(core, own, near_in, far_in)
    turns = [
        lax.ppermute(value, "zl", [(m, (m + turn + 1) % members) for m in range(members)])
        for turn, value in enumerate(turns)
    ]
    spread = pl.pallas_call(
        functools.partial(spread_kernel, 1 / math.sqrt(rows * groups * members)),
        out_shape=jax.ShapeDtypeStruct(parts.shape, jnp.bfloat16),
        in_specs=[vmem] + [anywhere],
        out_specs=vmem,
        compiler_params=params(),
        name="spread",
    )(folded, mine)
    parts = lax.all_to_all(spread, PLANE, 0, 0)
    feat_grad, weight_grad = pl.pallas_call(
        last_kernel,
        out_shape=(
            jax.ShapeDtypeStruct((rows, width), jnp.float32),
            jax.ShapeDtypeStruct(weight.shape, jnp.float32),
        ),
        in_specs=[vmem] * (members + 2),
        out_specs=(vmem, vmem),
        compiler_params=params(),
        name="last",
    )(mine, *turns, weight, parts)
    return (layer_out, feat_grad, weight_grad)


def solution(mesh):
    split = Mesh(mesh.devices.reshape(2, 8, 8, 2, 4), ALL)
    rows = P(ALL)
    return jax.shard_map(
        per_device,
        mesh=split,
        in_specs=(rows, rows, rows, rows, P(), rows),
        out_specs=(rows, rows, P()),
        check_vma=False,
    )
```
